32 devices in a mesh: chan: 8 (over z, y), win: 4 (over x, core).
Axes of the slice: x: 2, y: 2, z: 4, core: 2. Of those that a mesh axis runs over, the one named last changes fastest.
Arguments:
- strain: float32 [64, 32, 7500], P('chan', 'win'), may hold values from -800 to 800
- sources: int32 [4, 8], replicated, may hold values from 0 to 63, as said below
Outputs:
- stacks: float32 [32, 64, 513], P('win', 'chan')
The draws below stay inside these ranges and needn't reach their ends.
Inputs may be any that keep to these rules, and one draw needn't show every extreme that they name: `sources`: counting channels in aligned blocks of 8, the 8 channels of one round lie in different blocks, and over all rounds every block holds exactly 4 of them.
All inputs are finite; a program needn't handle non-finite values.
Results may differ from the reference program's by a relative error of at most 0.0024.
Values may be sent and summed in bfloat16 or wider, within the bound.
A program may use at most 128 MiB of HBM per device.

```python
import math
import jax
import jax.numpy as jnp
from jax import lax

CH_DEV = 8
SAMPLES = 7500
MAX_LAG = 256
SOURCES = 8
ROUNDS = 4
CHANNELS = 64
WINDOWS = 32


def draw_sources(key, part):
    owner_count = CHANNELS // CH_DEV
    shuffled = jax.random.permutation(jax.random.fold_in(key, 11), owner_count)
    owner_shards = shuffled[jnp.arange(ROUNDS * SOURCES) % owner_count]
    offsets = jax.random.randint(jax.random.fold_in(key, 12), (ROUNDS * SOURCES,), 0, CH_DEV)
    return (owner_shards * CH_DEV + offsets).astype(jnp.int32).reshape(ROUNDS, SOURCES)


def draw_strain(key, part):
    array_shape = (CHANNELS, WINDOWS, SAMPLES)
    envelope = jnp.exp(jax.random.uniform(jax.random.fold_in(key, 21), (1, WINDOWS, SAMPLES), jnp.float32) * math.log(10.0))
    row_level = jnp.exp(jax.random.uniform(jax.random.fold_in(key, 25), (CHANNELS, WINDOWS, 1), jnp.float32) * math.log(10.0))
    rough_part = jax.random.truncated_normal(jax.random.fold_in(key, 26), -4.0, 4.0, array_shape, jnp.float32)
    return row_level * envelope * rough_part


def setup_inputs(seed: int = 0) -> dict:
    keys = jax.random.split(jax.random.key(seed), 3)
    return {
        "strain": draw_strain(jax.random.fold_in(keys[2], 71), 0),
        "sources": draw_sources(jax.random.fold_in(keys[2], 71), 0),
    }


def whiten(strain):
    mean_square = lax.optimization_barrier(jnp.mean(strain * strain, axis=-1, keepdims=True))
    return (strain * lax.rsqrt(mean_square + 1e-06)).astype(jnp.bfloat16)

def receiver_rows(whitened, block_len):
    channels, windows, samples = whitened.shape
    blocks = -(-samples // block_len)
    padded = jnp.pad(whitened, ((0, 0), (0, 0), (0, blocks * block_len - samples)))
    pieces = padded.reshape(channels, windows, blocks, block_len)
    return jnp.transpose(pieces, (0, 3, 1, 2)).reshape(channels * block_len, windows * blocks)

def probe_columns(probe_rows, block_len, lag_blocks, max_lag):
    windows, samples = probe_rows.shape
    blocks = -(-samples // block_len)
    extent = (blocks + lag_blocks + 1) * block_len
    padded = jnp.pad(probe_rows, ((0, 0), (max_lag, extent - max_lag - samples)))
    pieces = padded.reshape(windows, blocks + lag_blocks + 1, block_len)
    stacked = jnp.stack([pieces[:, offset:offset + blocks, :] for offset in range(lag_blocks + 1)], axis=2)
    return stacked.reshape(windows * blocks, (lag_blocks + 1) * block_len)

def shear_sum(products, channels, block_len, lag_count):
    column_count = products.shape[1]
    flattened = products.reshape(channels, block_len * column_count)
    flattened = jnp.pad(flattened, ((0, 0), (0, block_len)))
    sheared = flattened.reshape(channels, block_len, column_count + 1)
    return lax.optimization_barrier(jnp.sum(sheared[:, :, :lag_count], axis=1))

def reference(strain, sources):
    whitened = whiten(strain)
    block_len = 64
    lag_count = 2 * MAX_LAG + 1
    lag_blocks = -(-lag_count // block_len)
    rows = receiver_rows(whitened, block_len).astype(jnp.float32)
    factor = 1.0 / math.sqrt(WINDOWS * SAMPLES)

    def correlate(channel):
        probe_rows = lax.dynamic_index_in_dim(whitened, channel, 0, keepdims=False)
        columns = probe_columns(probe_rows, block_len, lag_blocks, MAX_LAG).astype(jnp.float32)
        products = jnp.dot(rows, columns, precision=lax.Precision.HIGHEST, preferred_element_type=jnp.float32)
        return shear_sum(products, CHANNELS, block_len, lag_count) * factor
    return lax.map(correlate, sources.reshape(-1).astype(jnp.int32))
```

```python
import functools
import math

import jax
import jax.numpy as jnp
from jax import lax
from jax.experimental import pallas as pl
from jax.experimental.pallas import tpu as pltpu
from jax.sharding import PartitionSpec as P

MAX_LAG = 256
BLOCK = 128


def whiten(strain):
    mean_square = jnp.mean(strain * strain, axis=-1, keepdims=True)
    return (strain * lax.rsqrt(mean_square + 1e-06)).astype(jnp.bfloat16)


def correlate_kernel(factor, lag_blocks, order_ref, first_ref, second_ref, recv_ref, out_ref, probe_ref):
    channels = recv_ref.shape[0]
    depth = first_ref.shape[1]

    @pl.when(pl.program_id(0) == 0)
    def _():
        probe_ref[...] = jnp.zeros_like(probe_ref)

    probe_ref[:depth, :BLOCK] = first_ref[0]
    probe_ref[:depth, BLOCK:] = second_ref[0]
    row = lax.broadcasted_iota(jnp.int32, (BLOCK, BLOCK), 0)
    lane = lax.broadcasted_iota(jnp.int32, (BLOCK, BLOCK), 1)
    later = row + lane >= BLOCK - 1
    diagonal = row + lane == BLOCK - 1
    for channel in range(channels):
        products = jnp.dot(recv_ref[channel], probe_ref[...], preferred_element_type=jnp.float32)
        for half in range(2):
            columns = products[:, half * BLOCK : (half + 1) * BLOCK]
            parts = [columns[k * BLOCK : (k + 1) * BLOCK] for k in range(lag_blocks + 1)]
            for k in range(lag_blocks):
                mixed = jnp.where(later, parts[k], parts[k + 1])
                sheared = pltpu.roll(mixed, 0, 1, stride=1, stride_axis=0)
                total = jnp.sum(sheared, axis=0, keepdims=True)
                out_ref[half, channel : channel + 1, k * BLOCK : (k + 1) * BLOCK] = (
                    pltpu.roll(total, 1, 1) * factor
                )
            last = jnp.where(diagonal, parts[lag_blocks], 0.0)
            last = jnp.sum(jnp.sum(last, axis=0, keepdims=True), axis=1, keepdims=True)
            out_ref[half, channel : channel + 1, lag_blocks * BLOCK :] = last * factor


def correlate(gathered, receivers, order, factor):
    total, depth, _ = gathered.shape
    channels, rows, inner = receivers.shape
    lag_blocks = 2 * MAX_LAG // BLOCK
    lag_count = 2 * MAX_LAG + 1
    return pl.pallas_call(
        functools.partial(correlate_kernel, factor, lag_blocks),
        out_shape=jax.ShapeDtypeStruct((total, channels, lag_count), jnp.float32),
        grid_spec=pltpu.PrefetchScalarGridSpec(
            num_scalar_prefetch=1,
            grid=(total // 2,),
            in_specs=[
                pl.BlockSpec((1, depth, BLOCK), lambda p, order: (order[2 * p], 0, 0)),
                pl.BlockSpec((1, depth, BLOCK), lambda p, order: (order[2 * p + 1], 0, 0)),
                pl.BlockSpec((channels, rows, inner), lambda p, order: (0, 0, 0)),
            ],
            out_specs=pl.BlockSpec((2, channels, lag_count), lambda p, order: (p, 0, 0)),
            scratch_shapes=[pltpu.VMEM((inner, 2 * BLOCK), jnp.bfloat16)],
        ),
        compiler_params=pltpu.CompilerParams(vmem_limit_bytes=48 * 1024 * 1024),
    )(order, gathered, gathered, receivers)


def on_device(strain, sources):
    channels, windows, samples = strain.shape
    rounds, per_round = sources.shape
    total_sources = rounds * per_round
    lag_blocks = 2 * MAX_LAG // BLOCK
    ahead = MAX_LAG // BLOCK
    factor = 1.0 / math.sqrt(lax.axis_size("win") * windows * samples)
    blocks = -(-samples // BLOCK)
    while blocks * windows % 16:
        blocks += 1
    depth = blocks * windows
    inner = -(-depth // 256) * 256

    whitened = whiten(strain)
    padded = jnp.pad(whitened, ((0, 0), (0, 0), (0, blocks * BLOCK - samples)))
    pieces = padded.reshape(channels, windows, blocks, BLOCK)
    pieces = jnp.transpose(pieces, (0, 2, 1, 3)).reshape(channels, depth, BLOCK)

    flat_sources = sources.reshape(-1)
    per_shard = total_sources // lax.axis_size("chan")
    owner = flat_sources // channels
    position = jnp.arange(total_sources)
    earlier = (owner[None, :] == owner[:, None]) & (position[None, :] < position[:, None])
    rank = jnp.sum(earlier.astype(jnp.int32), axis=1)
    me = lax.axis_index("chan")
    mine = owner == me
    slot_pick = (mine[None, :] & (rank[None, :] == jnp.arange(per_shard)[:, None])).astype(jnp.int32)
    local_channel = jnp.sum(slot_pick * (flat_sources - me * channels)[None, :], axis=1)
    picked = jnp.concatenate(
        [lax.dynamic_slice_in_dim(pieces, local_channel[i], 1, 0) for i in range(per_shard)], axis=0
    )
    gathered = lax.all_gather(picked, "chan", axis=0, tiled=True)
    order = (owner * per_shard + rank).astype(jnp.int32)

    reverse = (jnp.arange(BLOCK)[:, None] + jnp.arange(BLOCK)[None, :] == BLOCK - 1).astype(jnp.bfloat16)
    flipped = lax.dot_general(
        pieces, reverse, (((2,), (1,)), ((), ())), preferred_element_type=jnp.float32
    ).astype(jnp.bfloat16)
    flipped = jnp.transpose(flipped, (0, 2, 1))
    front = (lag_blocks - ahead) * windows
    back = inner + lag_blocks * windows - front - depth
    flipped = jnp.pad(flipped, ((0, 0), (0, 0), (front, back)))
    receivers = jnp.concatenate(
        [
            flipped[:, :, (lag_blocks - k) * windows : (lag_blocks - k) * windows + inner]
            for k in range(lag_blocks + 1)
        ],
        axis=1,
    )
    partial_stack = correlate(gathered, receivers, order, factor)
    return lax.psum_scatter(partial_stack, "win", scatter_dimension=0, tiled=True)


def solution(mesh):
    in_specs = (P("chan", "win", None), P())
    out_specs = P("win", "chan", None)
    return jax.shard_map(
        on_device, mesh=mesh, in_specs=in_specs, out_specs=out_specs, check_vma=False
    )
```

```python
import functools
import math

import jax
import jax.numpy as jnp
from jax import lax
from jax.experimental import pallas as pl
from jax.experimental.pallas import tpu as pltpu
from jax.sharding import PartitionSpec as P

MAX_LAG = 256
BLOCK = 128


def whiten(strain):
    mean_square = jnp.mean(strain * strain, axis=-1, keepdims=True)
    return (strain * lax.rsqrt(mean_square + 1e-06)).astype(jnp.bfloat16)


def ring_position(index, size):
    odd = lax.rem(index, 2)
    half = index // 2
    return (1 - odd) * half + odd * (size - 1 - half)


def ring_index(position, size):
    back = position // (size // 2)
    return (1 - back) * 2 * position + back * (2 * (size - 1 - position) + 1)


def kernel(
    sizes, factor, picked_ref, recv_ref, order_ref, out_ref,
    held_ref, probe_ref, partial_ref, send_ref, land_ref,
    send_sem, recv_sem, stack_send_sem, stack_recv_sem,
):
    chan_size, win_size, lag_blocks = sizes
    channels = recv_ref.shape[0]
    ways, _, count, depth, _ = held_ref.shape
    per_shard = ways * count
    here = ring_position(lax.axis_index("chan"), chan_size)
    win = lax.axis_index("win")
    right = ring_index(lax.rem(here + 1, chan_size), chan_size)
    left = ring_index(lax.rem(here + chan_size - 1, chan_size), chan_size)
    targets = [right, left]

    barrier = pltpu.get_barrier_semaphore()
    for chan in targets:
        pl.semaphore_signal(barrier, inc=1, device_id={"chan": chan}, device_id_type=pl.DeviceIdType.MESH)
    for step in range(1, win_size):
        peer = lax.rem(win + step, win_size)
        pl.semaphore_signal(barrier, inc=1, device_id={"win": peer}, device_id_type=pl.DeviceIdType.MESH)
    for way in range(ways):
        held_ref[way, 0] = picked_ref[way * count : (way + 1) * count]
    probe_ref[...] = jnp.zeros_like(probe_ref)
    pl.semaphore_wait(barrier, len(targets) + win_size - 1)

    row = lax.broadcasted_iota(jnp.int32, (BLOCK, BLOCK), 0)
    lane = lax.broadcasted_iota(jnp.int32, (BLOCK, BLOCK), 1)
    later = row + lane >= BLOCK - 1
    diagonal = row + lane == BLOCK - 1

    def hop(way, step, item):
        return pltpu.make_async_remote_copy(
            src_ref=held_ref.at[way, step, item],
            dst_ref=held_ref.at[way, step + 1, item],
            send_sem=send_sem.at[way, step, item],
            recv_sem=recv_sem.at[way, step, item],
            device_id={"chan": targets[way]},
            device_id_type=pl.DeviceIdType.MESH,
        )

    def work(way, step):
        origin = here - step if way == 0 else here + step
        origin = ring_index(lax.rem(origin + chan_size, chan_size), chan_size)
        for item in range(count):
            probe_ref[way, :depth, item * BLOCK : (item + 1) * BLOCK] = held_ref[way, step, item]
        for channel in range(channels):
            products = jnp.dot(recv_ref[channel], probe_ref[way], preferred_element_type=jnp.float32)
            for item in range(count):
                columns = products[:, item * BLOCK : (item + 1) * BLOCK]
                parts = [columns[k * BLOCK : (k + 1) * BLOCK] for k in range(lag_blocks + 1)]
                totals = []
                for k in range(lag_blocks):
                    mixed = jnp.where(later, parts[k], parts[k + 1])
                    sheared = pltpu.roll(mixed, 0, 1, stride=1, stride_axis=0)
                    total = jnp.sum(sheared, axis=0, keepdims=True)
                    totals.append(pltpu.roll(total, 1, 1) * factor)
                last = jnp.where(diagonal, parts[lag_blocks], 0.0)
                last = jnp.sum(jnp.sum(last, axis=0, keepdims=True), axis=1, keepdims=True)
                totals.append(jnp.broadcast_to(last * factor, (1, BLOCK)))
                place = origin * per_shard + way * count + item
                partial_ref[place, channel : channel + 1, :] = jnp.concatenate(totals, axis=1)

    for way in range(ways):
        for item in range(count):
            hop(way, 0, item).start()

    slots = max(ways, count)

    def body(step, carry):
        for slot in range(slots):
            if slot < count:
                for way in range(ways):
                    hop(way, step - 1, slot).wait_recv()

                    @pl.when(step < chan_size - 1)
                    def _():
                        hop(way, step, slot).start()

            if slot < ways:
                work(slot, step - 1)
        return carry

    lax.fori_loop(1, chan_size, body, 0)
    for way in range(ways):
        work(way, chan_size - 1)
    for step in range(chan_size - 1):
        for way in range(ways):
            for item in range(count):
                hop(way, step, item).wait_send()

    per_win = out_ref.shape[0]
    for dest in range(win_size):
        for item in range(per_win):
            send_ref[dest, item] = partial_ref[order_ref[dest * per_win + item]]

    def stack_copy(step):
        peer = lax.rem(win + step, win_size)
        return pltpu.make_async_remote_copy(
            src_ref=send_ref.at[peer],
            dst_ref=land_ref.at[step - 1],
            send_sem=stack_send_sem.at[step - 1],
            recv_sem=stack_recv_sem.at[step - 1],
            device_id={"win": peer},
            device_id_type=pl.DeviceIdType.MESH,
        )

    for step in range(1, win_size):
        stack_copy(step).start()
    for step in range(1, win_size):
        stack_copy(step).wait_recv()
    total = send_ref[win]
    for step in range(1, win_size):
        total = total + land_ref[step - 1]
    out_ref[...] = total[:, :, : out_ref.shape[2]]
    for step in range(1, win_size):
        stack_copy(step).wait_send()


def correlate(picked, receivers, order, factor):
    per_shard, depth, _ = picked.shape
    channels, rows, inner = receivers.shape
    total = order.shape[0]
    chan_size, win_size = lax.axis_size("chan"), lax.axis_size("win")
    lag_blocks = 2 * MAX_LAG // BLOCK
    lag_count = 2 * MAX_LAG + 1
    lanes = (lag_blocks + 1) * BLOCK
    per_win = total // win_size
    ways = 2 if per_shard % 2 == 0 else 1
    count = per_shard // ways
    return pl.pallas_call(
        functools.partial(kernel, (chan_size, win_size, lag_blocks), factor),
        out_shape=jax.ShapeDtypeStruct((per_win, channels, lag_count), jnp.float32),
        in_specs=[
            pl.BlockSpec(memory_space=pltpu.VMEM),
            pl.BlockSpec(memory_space=pltpu.VMEM),
            pl.BlockSpec(memory_space=pltpu.SMEM),
        ],
        out_specs=pl.BlockSpec(memory_space=pltpu.VMEM),
        scratch_shapes=[
            pltpu.VMEM((ways, chan_size, count, depth, BLOCK), jnp.bfloat16),
            pltpu.VMEM((ways, inner, count * BLOCK), jnp.bfloat16),
            pltpu.VMEM((total, channels, lanes), jnp.float32),
            pltpu.VMEM((win_size, per_win, channels, lanes), jnp.float32),
            pltpu.VMEM((win_size - 1, per_win, channels, lanes), jnp.float32),
            pltpu.SemaphoreType.DMA((ways, chan_size - 1, count)),
            pltpu.SemaphoreType.DMA((ways, chan_size - 1, count)),
            pltpu.SemaphoreType.DMA((win_size - 1,)),
            pltpu.SemaphoreType.DMA((win_size - 1,)),
        ],
        compiler_params=pltpu.CompilerParams(
            vmem_limit_bytes=48 * 1024 * 1024, collective_id=0, has_side_effects=True
        ),
    )(picked, receivers, order)


def on_device(strain, sources):
    channels, windows, samples = strain.shape
    rounds, per_round = sources.shape
    total_sources = rounds * per_round
    lag_blocks = 2 * MAX_LAG // BLOCK
    ahead = MAX_LAG // BLOCK
    factor = 1.0 / math.sqrt(lax.axis_size("win") * windows * samples)
    blocks = -(-samples // BLOCK)
    while blocks * windows % 16:
        blocks += 1
    depth = blocks * windows
    inner = -(-depth // 256) * 256

    whitened = whiten(strain)
    padded = jnp.pad(whitened, ((0, 0), (0, 0), (0, blocks * BLOCK - samples)))
    pieces = padded.reshape(channels, windows, blocks, BLOCK)
    pieces = jnp.transpose(pieces, (0, 2, 1, 3)).reshape(channels, depth, BLOCK)

    flat_sources = sources.reshape(-1)
    per_shard = total_sources // lax.axis_size("chan")
    owner = flat_sources // channels
    position = jnp.arange(total_sources)
    earlier = (owner[None, :] == owner[:, None]) & (position[None, :] < position[:, None])
    rank = jnp.sum(earlier.astype(jnp.int32), axis=1)
    me = lax.axis_index("chan")
    mine = owner == me
    slot_pick = (mine[None, :] & (rank[None, :] == jnp.arange(per_shard)[:, None])).astype(jnp.int32)
    local_channel = jnp.sum(slot_pick * (flat_sources - me * channels)[None, :], axis=1)
    picked = jnp.concatenate(
        [lax.dynamic_slice_in_dim(pieces, local_channel[i], 1, 0) for i in range(per_shard)], axis=0
    )
    order = (owner * per_shard + rank).astype(jnp.int32)

    reverse = (jnp.arange(BLOCK)[:, None] + jnp.arange(BLOCK)[None, :] == BLOCK - 1).astype(jnp.bfloat16)
    flipped = lax.dot_general(
        pieces, reverse, (((2,), (1,)), ((), ())), preferred_element_type=jnp.float32
    ).astype(jnp.bfloat16)
    flipped = jnp.transpose(flipped, (0, 2, 1))
    front = (lag_blocks - ahead) * windows
    back = inner + lag_blocks * windows - front - depth
    flipped = jnp.pad(flipped, ((0, 0), (0, 0), (front, back)))
    receivers = jnp.concatenate(
        [
            flipped[:, :, (lag_blocks - k) * windows : (lag_blocks - k) * windows + inner]
            for k in range(lag_blocks + 1)
        ],
        axis=1,
    )
    return correlate(picked, receivers, order, factor)


def solution(mesh):
    in_specs = (P("chan", "win", None), P())
    out_specs = P("win", "chan", None)
    return jax.shard_map(
        on_device, mesh=mesh, in_specs=in_specs, out_specs=out_specs, check_vma=False
    )
```

```python
import functools
import math

import jax
import jax.numpy as jnp
from jax import lax
from jax.experimental import pallas as pl
from jax.experimental.pallas import tpu as pltpu
from jax.sharding import PartitionSpec as P

MAX_LAG = 256
BLOCK = 128


def whiten(strain):
    mean_square = jnp.mean(strain * strain, axis=-1, keepdims=True)
    return (strain * lax.rsqrt(mean_square + 1e-06)).astype(jnp.bfloat16)


def ring_position(index, size):
    odd = lax.rem(index, 2)
    half = index // 2
    return (1 - odd) * half + odd * (size - 1 - half)


def ring_index(position, size):
    back = position // (size // 2)
    return (1 - back) * 2 * position + back * (2 * (size - 1 - position) + 1)


def kernel(
    sizes, factor, pieces_ref, local_ref, order_ref, out_ref,
    recv_ref, wide_ref, held_ref, probe_ref, partial_ref, send_ref, land_ref,
    send_sem, recv_sem, stack_send_sem, stack_recv_sem,
):
    chan_size, win_size, lag_blocks, windows, front = sizes
    channels = recv_ref.shape[0]
    ways, _, count, depth, _ = held_ref.shape
    per_shard = ways * count
    here = ring_position(lax.axis_index("chan"), chan_size)
    win = lax.axis_index("win")
    right = ring_index(lax.rem(here + 1, chan_size), chan_size)
    left = ring_index(lax.rem(here + chan_size - 1, chan_size), chan_size)
    targets = [right, left]

    barrier = pltpu.get_barrier_semaphore()
    for chan in targets:
        pl.semaphore_signal(barrier, inc=1, device_id={"chan": chan}, device_id_type=pl.DeviceIdType.MESH)
    for step in range(1, win_size):
        peer = lax.rem(win + step, win_size)
        pl.semaphore_signal(barrier, inc=1, device_id={"win": peer}, device_id_type=pl.DeviceIdType.MESH)
    for way in range(ways):
        for item in range(count):
            held_ref[way, 0, item] = pieces_ref[local_ref[way * count + item]]
    probe_ref[...] = jnp.zeros_like(probe_ref)
    pl.semaphore_wait(barrier, len(targets) + win_size - 1)

    row = lax.broadcasted_iota(jnp.int32, (BLOCK, BLOCK), 0)
    lane = lax.broadcasted_iota(jnp.int32, (BLOCK, BLOCK), 1)
    later = row + lane >= BLOCK - 1
    diagonal = row + lane == BLOCK - 1

    def hop(way, step, item):
        return pltpu.make_async_remote_copy(
            src_ref=held_ref.at[way, step, item],
            dst_ref=held_ref.at[way, step + 1, item],
            send_sem=send_sem.at[way, step, item],
            recv_sem=recv_sem.at[way, step, item],
            device_id={"chan": targets[way]},
            device_id_type=pl.DeviceIdType.MESH,
        )

    def work(way, step):
        origin = here - step if way == 0 else here + step
        origin = ring_index(lax.rem(origin + chan_size, chan_size), chan_size)
        for item in range(count):
            probe_ref[way, :depth, item * BLOCK : (item + 1) * BLOCK] = held_ref[way, step, item]
        for channel in range(channels):
            products = jnp.dot(recv_ref[channel], probe_ref[way], preferred_element_type=jnp.float32)
            for item in range(count):
                columns = products[:, item * BLOCK : (item + 1) * BLOCK]
                parts = [columns[k * BLOCK : (k + 1) * BLOCK] for k in range(lag_blocks + 1)]
                totals = []
                for k in range(lag_blocks):
                    mixed = jnp.where(later, parts[k], parts[k + 1])
                    sheared = pltpu.roll(mixed, 0, 1, stride=1, stride_axis=0)
                    total = jnp.sum(sheared, axis=0, keepdims=True)
                    totals.append(pltpu.roll(total, 1, 1) * factor)
                last = jnp.where(diagonal, parts[lag_blocks], 0.0)
                last = jnp.sum(jnp.sum(last, axis=0, keepdims=True), axis=1, keepdims=True)
                totals.append(jnp.broadcast_to(last * factor, (1, BLOCK)))
                place = origin * per_shard + way * count + item
                partial_ref[place, channel : channel + 1, :] = jnp.concatenate(totals, axis=1)

    for way in range(ways):
        for item in range(count):
            hop(way, 0, item).start()

    reverse = jnp.where(diagonal, 1.0, 0.0).astype(jnp.bfloat16)
    inner = recv_ref.shape[2]
    reach = wide_ref.shape[1]
    wide_ref[...] = jnp.zeros_like(wide_ref)
    for channel in range(channels):
        wide_ref[channel % 2, front : front + depth, :] = pieces_ref[channel]
        flipped = lax.dot_general(
            reverse, wide_ref[channel % 2], (((1,), (1,)), ((), ())), preferred_element_type=jnp.float32
        )
        for k in range(lag_blocks + 1):
            shift = (lag_blocks - k) * windows
            moved = pltpu.roll(flipped, reach - shift, 1) if shift else flipped
            recv_ref[channel, k * BLOCK : (k + 1) * BLOCK, :] = moved[:, :inner].astype(jnp.bfloat16)

    slots = max(ways, count)

    def body(step, carry):
        for slot in range(slots):
            if slot < count:
                for way in range(ways):
                    hop(way, step - 1, slot).wait_recv()

                    @pl.when(step < chan_size - 1)
                    def _():
                        hop(way, step, slot).start()

            if slot < ways:
                work(slot, step - 1)
        return carry

    lax.fori_loop(1, chan_size, body, 0)
    for way in range(ways):
        work(way, chan_size - 1)
    for step in range(chan_size - 1):
        for way in range(ways):
            for item in range(count):
                hop(way, step, item).wait_send()

    per_win = out_ref.shape[0]
    for dest in range(win_size):
        for item in range(per_win):
            send_ref[dest, item] = partial_ref[order_ref[dest * per_win + item]]

    def stack_copy(step):
        peer = lax.rem(win + step, win_size)
        return pltpu.make_async_remote_copy(
            src_ref=send_ref.at[peer],
            dst_ref=land_ref.at[step - 1],
            send_sem=stack_send_sem.at[step - 1],
            recv_sem=stack_recv_sem.at[step - 1],
            device_id={"win": peer},
            device_id_type=pl.DeviceIdType.MESH,
        )

    for step in range(1, win_size):
        stack_copy(step).start()
    for step in range(1, win_size):
        stack_copy(step).wait_recv()
    total = send_ref[win]
    for step in range(1, win_size):
        total = total + land_ref[step - 1]
    out_ref[...] = total[:, :, : out_ref.shape[2]]
    for step in range(1, win_size):
        stack_copy(step).wait_send()


def correlate(pieces, local_channel, order, windows, factor):
    channels, depth, _ = pieces.shape
    per_shard = local_channel.shape[0]
    total = order.shape[0]
    chan_size, win_size = lax.axis_size("chan"), lax.axis_size("win")
    lag_blocks = 2 * MAX_LAG // BLOCK
    lag_count = 2 * MAX_LAG + 1
    front = (lag_blocks - MAX_LAG // BLOCK) * windows
    inner = -(-depth // 256) * 256
    reach = -(-(inner + lag_blocks * windows) // BLOCK) * BLOCK
    lanes = (lag_blocks + 1) * BLOCK
    per_win = total // win_size
    ways = 2 if per_shard % 2 == 0 else 1
    count = per_shard // ways
    return pl.pallas_call(
        functools.partial(kernel, (chan_size, win_size, lag_blocks, windows, front), factor),
        out_shape=jax.ShapeDtypeStruct((per_win, channels, lag_count), jnp.float32),
        in_specs=[
            pl.BlockSpec(memory_space=pltpu.VMEM),
            pl.BlockSpec(memory_space=pltpu.SMEM),
            pl.BlockSpec(memory_space=pltpu.SMEM),
        ],
        out_specs=pl.BlockSpec(memory_space=pltpu.VMEM),
        scratch_shapes=[
            pltpu.VMEM((channels, (lag_blocks + 1) * BLOCK, inner), jnp.bfloat16),
            pltpu.VMEM((2, reach, BLOCK), jnp.bfloat16),
            pltpu.VMEM((ways, chan_size, count, depth, BLOCK), jnp.bfloat16),
            pltpu.VMEM((ways, inner, count * BLOCK), jnp.bfloat16),
            pltpu.VMEM((total, channels, lanes), jnp.float32),
            pltpu.VMEM((win_size, per_win, channels, lanes), jnp.float32),
            pltpu.VMEM((win_size - 1, per_win, channels, lanes), jnp.float32),
            pltpu.SemaphoreType.DMA((ways, chan_size - 1, count)),
            pltpu.SemaphoreType.DMA((ways, chan_size - 1, count)),
            pltpu.SemaphoreType.DMA((win_size - 1,)),
            pltpu.SemaphoreType.DMA((win_size - 1,)),
        ],
        compiler_params=pltpu.CompilerParams(
            vmem_limit_bytes=48 * 1024 * 1024, collective_id=0, has_side_effects=True
        ),
    )(pieces, local_channel, order)


def on_device(strain, sources):
    channels, windows, samples = strain.shape
    rounds, per_round = sources.shape
    total_sources = rounds * per_round
    factor = 1.0 / math.sqrt(lax.axis_size("win") * windows * samples)
    blocks = -(-samples // BLOCK)
    while blocks * windows % 16:
        blocks += 1
    depth = blocks * windows

    whitened = whiten(strain)
    padded = jnp.pad(whitened, ((0, 0), (0, 0), (0, blocks * BLOCK - samples)))
    pieces = padded.reshape(channels, windows, blocks, BLOCK)
    pieces = jnp.transpose(pieces, (0, 2, 1, 3)).reshape(channels, depth, BLOCK)

    flat_sources = sources.reshape(-1)
    per_shard = total_sources // lax.axis_size("chan")
    owner = flat_sources // channels
    position = jnp.arange(total_sources)
    earlier = (owner[None, :] == owner[:, None]) & (position[None, :] < position[:, None])
    rank = jnp.sum(earlier.astype(jnp.int32), axis=1)
    me = lax.axis_index("chan")
    mine = owner == me
    slot_pick = (mine[None, :] & (rank[None, :] == jnp.arange(per_shard)[:, None])).astype(jnp.int32)
    local_channel = jnp.sum(slot_pick * (flat_sources - me * channels)[None, :], axis=1)
    order = (owner * per_shard + rank).astype(jnp.int32)

    return correlate(pieces, local_channel.astype(jnp.int32), order, windows, factor)


def solution(mesh):
    in_specs = (P("chan", "win", None), P())
    out_specs = P("win", "chan", None)
    return jax.shard_map(
        on_device, mesh=mesh, in_specs=in_specs, out_specs=out_specs, check_vma=False
    )
```

```python
import functools
import math

import jax
import jax.numpy as jnp
from jax import lax
from jax.experimental import pallas as pl
from jax.experimental.pallas import tpu as pltpu
from jax.sharding import PartitionSpec as P

MAX_LAG = 256
BLOCK = 128


def whiten(strain):
    mean_square = jnp.mean(strain * strain, axis=-1, keepdims=True)
    return (strain * lax.rsqrt(mean_square + 1e-06)).astype(jnp.bfloat16)


def ring_position(index, size):
    odd = lax.rem(index, 2)
    half = index // 2
    return (1 - odd) * half + odd * (size - 1 - half)


def ring_index(position, size):
    back = position // (size // 2)
    return (1 - back) * 2 * position + back * (2 * (size - 1 - position) + 1)


def kernel(
    sizes, streamed, factor, pieces_ref, local_ref, order_ref, out_ref,
    recv_ref, wide_ref, held_ref, probe_ref, partial_ref, send_ref, land_ref,
    send_sem, recv_sem, stack_send_sem, stack_recv_sem,
):
    chan_size, win_size, lag_blocks, windows, front = sizes
    channels = recv_ref.shape[0]
    ways, _, count, depth, _ = held_ref.shape
    per_shard = ways * count
    here = ring_position(lax.axis_index("chan"), chan_size)
    win = lax.axis_index("win")
    right = ring_index(lax.rem(here + 1, chan_size), chan_size)
    left = ring_index(lax.rem(here + chan_size - 1, chan_size), chan_size)
    targets = [right, left]

    barrier = pltpu.get_barrier_semaphore()
    for chan in targets:
        pl.semaphore_signal(barrier, inc=1, device_id={"chan": chan}, device_id_type=pl.DeviceIdType.MESH)
    for step in range(1, win_size):
        peer = lax.rem(win + step, win_size)
        pl.semaphore_signal(barrier, inc=1, device_id={"win": peer}, device_id_type=pl.DeviceIdType.MESH)
    for way in range(ways):
        for item in range(count):
            held_ref[way, 0, item] = pieces_ref[local_ref[way * count + item]]
    probe_ref[...] = jnp.zeros_like(probe_ref)
    pl.semaphore_wait(barrier, len(targets) + win_size - 1)

    row = lax.broadcasted_iota(jnp.int32, (BLOCK, BLOCK), 0)
    lane = lax.broadcasted_iota(jnp.int32, (BLOCK, BLOCK), 1)
    later = row + lane >= BLOCK - 1
    diagonal = row + lane == BLOCK - 1

    def hop(way, step, item):
        return pltpu.make_async_remote_copy(
            src_ref=held_ref.at[way, step, item],
            dst_ref=held_ref.at[way, step + 1, item],
            send_sem=send_sem.at[way, step, item],
            recv_sem=recv_sem.at[way, step, item],
            device_id={"chan": targets[way]},
            device_id_type=pl.DeviceIdType.MESH,
        )

    def stack_hop(dest, origin):
        slot = lax.rem(dest - win + win_size, win_size) - 1
        return pltpu.make_async_remote_copy(
            src_ref=partial_ref.at[origin * per_shard + dest],
            dst_ref=land_ref.at[slot, origin],
            send_sem=stack_send_sem.at[dest, origin],
            recv_sem=stack_recv_sem.at[slot, origin],
            device_id={"win": jnp.int32(dest)},
            device_id_type=pl.DeviceIdType.MESH,
        )

    def work(way, step):
        origin = here - step if way == 0 else here + step
        origin = ring_index(lax.rem(origin + chan_size, chan_size), chan_size)
        for item in range(count):
            probe_ref[way, :depth, item * BLOCK : (item + 1) * BLOCK] = held_ref[way, step, item]
        for channel in range(channels):
            products = jnp.dot(recv_ref[channel], probe_ref[way], preferred_element_type=jnp.float32)
            for item in range(count):
                columns = products[:, item * BLOCK : (item + 1) * BLOCK]
                parts = [columns[k * BLOCK : (k + 1) * BLOCK] for k in range(lag_blocks + 1)]
                totals = []
                for k in range(lag_blocks):
                    mixed = jnp.where(later, parts[k], parts[k + 1])
                    sheared = pltpu.roll(mixed, 0, 1, stride=1, stride_axis=0)
                    total = jnp.sum(sheared, axis=0, keepdims=True)
                    totals.append(pltpu.roll(total, 1, 1) * factor)
                last = jnp.where(diagonal, parts[lag_blocks], 0.0)
                last = jnp.sum(jnp.sum(last, axis=0, keepdims=True), axis=1, keepdims=True)
                totals.append(jnp.broadcast_to(last * factor, (1, BLOCK)))
                place = origin * per_shard + way * count + item
                partial_ref[place, channel : channel + 1, :] = jnp.concatenate(totals, axis=1)
        if streamed:
            for item in range(count):
                dest = way * count + item

                @pl.when(win != dest)
                def _():
                    stack_hop(dest, origin).start()

    for way in range(ways):
        for item in range(count):
            hop(way, 0, item).start()

    reverse = jnp.where(diagonal, 1.0, 0.0).astype(jnp.bfloat16)
    inner = recv_ref.shape[2]
    reach = wide_ref.shape[1]
    wide_ref[...] = jnp.zeros_like(wide_ref)
    for channel in range(channels):
        wide_ref[channel % 2, front : front + depth, :] = pieces_ref[channel]
        flipped = lax.dot_general(
            reverse, wide_ref[channel % 2], (((1,), (1,)), ((), ())), preferred_element_type=jnp.float32
        )
        for k in range(lag_blocks + 1):
            shift = (lag_blocks - k) * windows
            moved = pltpu.roll(flipped, reach - shift, 1) if shift else flipped
            recv_ref[channel, k * BLOCK : (k + 1) * BLOCK, :] = moved[:, :inner].astype(jnp.bfloat16)

    slots = max(ways, count)

    def body(step, carry):
        for slot in range(slots):
            if slot < count:
                for way in range(ways):
                    hop(way, step - 1, slot).wait_recv()

                    @pl.when(step < chan_size - 1)
                    def _():
                        hop(way, step, slot).start()

            if slot < ways:
                work(slot, step - 1)
        return carry

    lax.fori_loop(1, chan_size, body, 0)
    for way in range(ways):
        work(way, chan_size - 1)
    for step in range(chan_size - 1):
        for way in range(ways):
            for item in range(count):
                hop(way, step, item).wait_send()

    per_win = out_ref.shape[0]
    if streamed:
        def arrived(index, carry):
            for slot in range(win_size - 1):
                peer = lax.rem(win + slot + 1, win_size)
                pltpu.make_async_remote_copy(
                    src_ref=partial_ref.at[index],
                    dst_ref=land_ref.at[slot, index],
                    send_sem=stack_send_sem.at[slot, index],
                    recv_sem=stack_recv_sem.at[slot, index],
                    device_id={"win": peer},
                    device_id_type=pl.DeviceIdType.MESH,
                ).wait_recv()
            return carry

        lax.fori_loop(0, chan_size, arrived, 0)
        for item in range(per_win):
            place = order_ref[win * per_win + item]
            owner = lax.div(place, per_shard)
            total = partial_ref[place]
            for slot in range(win_size - 1):
                total = total + land_ref[slot, owner]
            out_ref[item] = total[:, : out_ref.shape[2]]

        def sent(index, carry):
            for dest in range(win_size):
                @pl.when(win != dest)
                def _():
                    stack_hop(dest, index).wait_send()
            return carry

        lax.fori_loop(0, chan_size, sent, 0)
        return

    for dest in range(win_size):
        for item in range(per_win):
            send_ref[dest, item] = partial_ref[order_ref[dest * per_win + item]]

    def stack_copy(step):
        peer = lax.rem(win + step, win_size)
        return pltpu.make_async_remote_copy(
            src_ref=send_ref.at[peer],
            dst_ref=land_ref.at[step - 1],
            send_sem=stack_send_sem.at[step - 1],
            recv_sem=stack_recv_sem.at[step - 1],
            device_id={"win": peer},
            device_id_type=pl.DeviceIdType.MESH,
        )

    for step in range(1, win_size):
        stack_copy(step).start()
    for step in range(1, win_size):
        stack_copy(step).wait_recv()
    total = send_ref[win]
    for step in range(1, win_size):
        total = total + land_ref[step - 1]
    out_ref[...] = total[:, :, : out_ref.shape[2]]
    for step in range(1, win_size):
        stack_copy(step).wait_send()


def correlate(pieces, local_channel, order, windows, rounds, factor):
    channels, depth, _ = pieces.shape
    per_shard = local_channel.shape[0]
    total = order.shape[0]
    chan_size, win_size = lax.axis_size("chan"), lax.axis_size("win")
    lag_blocks = 2 * MAX_LAG // BLOCK
    lag_count = 2 * MAX_LAG + 1
    front = (lag_blocks - MAX_LAG // BLOCK) * windows
    inner = -(-depth // 256) * 256
    reach = -(-(inner + lag_blocks * windows) // BLOCK) * BLOCK
    lanes = (lag_blocks + 1) * BLOCK
    per_win = total // win_size
    streamed = rounds == win_size and total // rounds == chan_size and per_shard == rounds
    stack_copies = (win_size, chan_size) if streamed else (win_size - 1,)
    ways = 2 if per_shard % 2 == 0 else 1
    count = per_shard // ways
    return pl.pallas_call(
        functools.partial(kernel, (chan_size, win_size, lag_blocks, windows, front), streamed, factor),
        out_shape=jax.ShapeDtypeStruct((per_win, channels, lag_count), jnp.float32),
        in_specs=[
            pl.BlockSpec(memory_space=pltpu.VMEM),
            pl.BlockSpec(memory_space=pltpu.SMEM),
            pl.BlockSpec(memory_space=pltpu.SMEM),
        ],
        out_specs=pl.BlockSpec(memory_space=pltpu.VMEM),
        scratch_shapes=[
            pltpu.VMEM((channels, (lag_blocks + 1) * BLOCK, inner), jnp.bfloat16),
            pltpu.VMEM((2, reach, BLOCK), jnp.bfloat16),
            pltpu.VMEM((ways, chan_size, count, depth, BLOCK), jnp.bfloat16),
            pltpu.VMEM((ways, inner, count * BLOCK), jnp.bfloat16),
            pltpu.VMEM((total, channels, lanes), jnp.float32),
            pltpu.VMEM((win_size, per_win, channels, lanes), jnp.float32),
            pltpu.VMEM((win_size - 1, per_win, channels, lanes), jnp.float32),
            pltpu.SemaphoreType.DMA((ways, chan_size - 1, count)),
            pltpu.SemaphoreType.DMA((ways, chan_size - 1, count)),
            pltpu.SemaphoreType.DMA(stack_copies),
            pltpu.SemaphoreType.DMA(stack_copies),
        ],
        compiler_params=pltpu.CompilerParams(
            vmem_limit_bytes=48 * 1024 * 1024, collective_id=0, has_side_effects=True
        ),
    )(pieces, local_channel, order)


def on_device(strain, sources):
    channels, windows, samples = strain.shape
    rounds, per_round = sources.shape
    total_sources = rounds * per_round
    factor = 1.0 / math.sqrt(lax.axis_size("win") * windows * samples)
    blocks = -(-samples // BLOCK)
    while blocks * windows % 16:
        blocks += 1
    depth = blocks * windows

    whitened = whiten(strain)
    padded = jnp.pad(whitened, ((0, 0), (0, 0), (0, blocks * BLOCK - samples)))
    pieces = padded.reshape(channels, windows, blocks, BLOCK)
    pieces = jnp.transpose(pieces, (0, 2, 1, 3)).reshape(channels, depth, BLOCK)

    flat_sources = sources.reshape(-1)
    per_shard = total_sources // lax.axis_size("chan")
    owner = flat_sources // channels
    position = jnp.arange(total_sources)
    earlier = (owner[None, :] == owner[:, None]) & (position[None, :] < position[:, None])
    rank = jnp.sum(earlier.astype(jnp.int32), axis=1)
    me = lax.axis_index("chan")
    mine = owner == me
    slot_pick = (mine[None, :] & (rank[None, :] == jnp.arange(per_shard)[:, None])).astype(jnp.int32)
    local_channel = jnp.sum(slot_pick * (flat_sources - me * channels)[None, :], axis=1)
    order = (owner * per_shard + rank).astype(jnp.int32)

    return correlate(pieces, local_channel.astype(jnp.int32), order, windows, rounds, factor)


def solution(mesh):
    in_specs = (P("chan", "win", None), P())
    out_specs = P("win", "chan", None)
    return jax.shard_map(
        on_device, mesh=mesh, in_specs=in_specs, out_specs=out_specs, check_vma=False
    )
```

```python
import functools
import math

import jax
import jax.numpy as jnp
from jax import lax
from jax.experimental import pallas as pl
from jax.experimental.pallas import tpu as pltpu
from jax.sharding import PartitionSpec as P

MAX_LAG = 256
BLOCK = 128


def whiten(strain):
    mean_square = jnp.mean(strain * strain, axis=-1, keepdims=True)
    return (strain * lax.rsqrt(mean_square + 1e-06)).astype(jnp.bfloat16)


def ring_position(index, size):
    odd = lax.rem(index, 2)
    half = index // 2
    return (1 - odd) * half + odd * (size - 1 - half)


def ring_index(position, size):
    back = position // (size // 2)
    return (1 - back) * 2 * position + back * (2 * (size - 1 - position) + 1)


def kernel(
    sizes, streamed, factor, pieces_ref, local_ref, order_ref, out_ref,
    recv_ref, wide_ref, held_ref, own_ref, probe_ref, partial_ref, send_ref, land_ref,
    send_sem, recv_sem, stack_send_sem, stack_recv_sem,
):
    chan_size, win_size, lag_blocks, windows, front = sizes
    channels = recv_ref.shape[0]
    ways, _, count, depth, _ = held_ref.shape
    per_shard = ways * count
    here = ring_position(lax.axis_index("chan"), chan_size)
    win = lax.axis_index("win")
    right = ring_index(lax.rem(here + 1, chan_size), chan_size)
    left = ring_index(lax.rem(here + chan_size - 1, chan_size), chan_size)
    targets = [right, left]

    barrier = pltpu.get_barrier_semaphore()
    for chan in targets:
        pl.semaphore_signal(barrier, inc=1, device_id={"chan": chan}, device_id_type=pl.DeviceIdType.MESH)
    for step in range(1, win_size):
        peer = lax.rem(win + step, win_size)
        pl.semaphore_signal(barrier, inc=1, device_id={"win": peer}, device_id_type=pl.DeviceIdType.MESH)
    for way in range(ways):
        for item in range(count):
            held_ref[way, 0, item] = pieces_ref[local_ref[way * count + item]]
    own_ref[...] = jnp.zeros_like(own_ref)
    probe_ref[...] = jnp.zeros_like(probe_ref)
    pl.semaphore_wait(barrier, len(targets) + win_size - 1)

    row = lax.broadcasted_iota(jnp.int32, (BLOCK, BLOCK), 0)
    lane = lax.broadcasted_iota(jnp.int32, (BLOCK, BLOCK), 1)
    later = row + lane >= BLOCK - 1
    diagonal = row + lane == BLOCK - 1

    def hop(way, step, item):
        return pltpu.make_async_remote_copy(
            src_ref=held_ref.at[way, step, item],
            dst_ref=held_ref.at[way, step + 1, item],
            send_sem=send_sem.at[way, step, item],
            recv_sem=recv_sem.at[way, step, item],
            device_id={"chan": targets[way]},
            device_id_type=pl.DeviceIdType.MESH,
        )

    def stack_hop(dest, origin):
        slot = lax.rem(dest - win + win_size, win_size) - 1
        return pltpu.make_async_remote_copy(
            src_ref=partial_ref.at[origin * per_shard + dest],
            dst_ref=land_ref.at[slot, origin],
            send_sem=stack_send_sem.at[dest, origin],
            recv_sem=stack_recv_sem.at[slot, origin],
            device_id={"win": jnp.int32(dest)},
            device_id_type=pl.DeviceIdType.MESH,
        )

    def origin_of(way, step):
        position = here - step if way == 0 else here + step
        return ring_index(lax.rem(position + chan_size, chan_size), chan_size)

    def load(probe, item, step):
        for way in range(ways):
            probe[item, :depth, way * BLOCK : (way + 1) * BLOCK] = held_ref[way, step, item]

    def work(probe, item, step, channel):
        products = jnp.dot(recv_ref[channel], probe[item], preferred_element_type=jnp.float32)
        for way in range(ways):
            columns = products[:, way * BLOCK : (way + 1) * BLOCK]
            parts = [columns[k * BLOCK : (k + 1) * BLOCK] for k in range(lag_blocks + 1)]
            totals = []
            for k in range(lag_blocks):
                mixed = jnp.where(later, parts[k], parts[k + 1])
                sheared = pltpu.roll(mixed, 0, 1, stride=1, stride_axis=0)
                total = jnp.sum(sheared, axis=0, keepdims=True)
                totals.append(pltpu.roll(total, 1, 1) * factor)
            last = jnp.where(diagonal, parts[lag_blocks], 0.0)
            last = jnp.sum(jnp.sum(last, axis=0, keepdims=True), axis=1, keepdims=True)
            totals.append(jnp.broadcast_to(last * factor, (1, BLOCK)))
            place = origin_of(way, step) * per_shard + way * count + item
            partial_ref[place, pl.ds(channel, 1), :] = jnp.concatenate(totals, axis=1)

    def send_stacks(item, step):
        if not streamed:
            return
        for way in range(ways):
            dest = way * count + item

            @pl.when(win != dest)
            def _():
                stack_hop(dest, origin_of(way, step)).start()

    for way in range(ways):
        for item in range(count):
            hop(way, 0, item).start()

    reverse = jnp.where(diagonal, 1.0, 0.0).astype(jnp.bfloat16)
    inner = recv_ref.shape[2]
    reach = wide_ref.shape[1]
    wide_ref[...] = jnp.zeros_like(wide_ref)
    for channel in range(channels):
        wide_ref[channel % 2, front : front + depth, :] = pieces_ref[channel]
        flipped = lax.dot_general(
            reverse, wide_ref[channel % 2], (((1,), (1,)), ((), ())), preferred_element_type=jnp.float32
        )
        for k in range(lag_blocks + 1):
            shift = (lag_blocks - k) * windows
            moved = pltpu.roll(flipped, reach - shift, 1) if shift else flipped
            recv_ref[channel, k * BLOCK : (k + 1) * BLOCK, :] = moved[:, :inner].astype(jnp.bfloat16)

    spread = chan_size - 1 if chan_size - 1 <= channels else 0
    for item in range(count):
        load(own_ref, item, 0)
        for channel in range(channels - spread):
            work(own_ref, item, 0, channel)

    def body(step, carry):
        for item in range(count):
            for way in range(ways):
                hop(way, step - 1, item).wait_recv()

                @pl.when(step < chan_size - 1)
                def _():
                    hop(way, step, item).start()

            load(probe_ref, item, step)
            if spread:
                work(own_ref, item, 0, channels - spread + step - 1)
            for channel in range(channels):
                work(probe_ref, item, step, channel)
            send_stacks(item, step)
        return carry

    lax.fori_loop(1, chan_size, body, 0)
    for item in range(count):
        send_stacks(item, 0)
    for step in range(chan_size - 1):
        for way in range(ways):
            for item in range(count):
                hop(way, step, item).wait_send()

    per_win = out_ref.shape[0]
    if streamed:
        def arrived(index, carry):
            for slot in range(win_size - 1):
                peer = lax.rem(win + slot + 1, win_size)
                pltpu.make_async_remote_copy(
                    src_ref=partial_ref.at[index],
                    dst_ref=land_ref.at[slot, index],
                    send_sem=stack_send_sem.at[slot, index],
                    recv_sem=stack_recv_sem.at[slot, index],
                    device_id={"win": peer},
                    device_id_type=pl.DeviceIdType.MESH,
                ).wait_recv()
            return carry

        lax.fori_loop(0, chan_size, arrived, 0)
        for item in range(per_win):
            place = order_ref[win * per_win + item]
            owner = lax.div(place, per_shard)
            total = partial_ref[place]
            for slot in range(win_size - 1):
                total = total + land_ref[slot, owner]
            out_ref[item] = total[:, : out_ref.shape[2]]

        def sent(index, carry):
            for dest in range(win_size):
                @pl.when(win != dest)
                def _():
                    stack_hop(dest, index).wait_send()
            return carry

        lax.fori_loop(0, chan_size, sent, 0)
        return

    for dest in range(win_size):
        for item in range(per_win):
            send_ref[dest, item] = partial_ref[order_ref[dest * per_win + item]]

    def stack_copy(step):
        peer = lax.rem(win + step, win_size)
        return pltpu.make_async_remote_copy(
            src_ref=send_ref.at[peer],
            dst_ref=land_ref.at[step - 1],
            send_sem=stack_send_sem.at[step - 1],
            recv_sem=stack_recv_sem.at[step - 1],
            device_id={"win": peer},
            device_id_type=pl.DeviceIdType.MESH,
        )

    for step in range(1, win_size):
        stack_copy(step).start()
    for step in range(1, win_size):
        stack_copy(step).wait_recv()
    total = send_ref[win]
    for step in range(1, win_size):
        total = total + land_ref[step - 1]
    out_ref[...] = total[:, :, : out_ref.shape[2]]
    for step in range(1, win_size):
        stack_copy(step).wait_send()


def correlate(pieces, local_channel, order, windows, rounds, factor):
    channels, depth, _ = pieces.shape
    per_shard = local_channel.shape[0]
    total = order.shape[0]
    chan_size, win_size = lax.axis_size("chan"), lax.axis_size("win")
    lag_blocks = 2 * MAX_LAG // BLOCK
    lag_count = 2 * MAX_LAG + 1
    front = (lag_blocks - MAX_LAG // BLOCK) * windows
    inner = -(-depth // 256) * 256
    reach = -(-(inner + lag_blocks * windows) // BLOCK) * BLOCK
    lanes = (lag_blocks + 1) * BLOCK
    per_win = total // win_size
    streamed = rounds == win_size and total // rounds == chan_size and per_shard == rounds
    stack_copies = (win_size, chan_size) if streamed else (win_size - 1,)
    ways = 2 if per_shard % 2 == 0 else 1
    count = per_shard // ways
    return pl.pallas_call(
        functools.partial(kernel, (chan_size, win_size, lag_blocks, windows, front), streamed, factor),
        out_shape=jax.ShapeDtypeStruct((per_win, channels, lag_count), jnp.float32),
        in_specs=[
            pl.BlockSpec(memory_space=pltpu.VMEM),
            pl.BlockSpec(memory_space=pltpu.SMEM),
            pl.BlockSpec(memory_space=pltpu.SMEM),
        ],
        out_specs=pl.BlockSpec(memory_space=pltpu.VMEM),
        scratch_shapes=[
            pltpu.VMEM((channels, (lag_blocks + 1) * BLOCK, inner), jnp.bfloat16),
            pltpu.VMEM((2, reach, BLOCK), jnp.bfloat16),
            pltpu.VMEM((ways, chan_size, count, depth, BLOCK), jnp.bfloat16),
            pltpu.VMEM((count, inner, ways * BLOCK), jnp.bfloat16),
            pltpu.VMEM((count, inner, ways * BLOCK), jnp.bfloat16),
            pltpu.VMEM((total, channels, lanes), jnp.float32),
            pltpu.VMEM((win_size, per_win, channels, lanes), jnp.float32),
            pltpu.VMEM((win_size - 1, per_win, channels, lanes), jnp.float32),
            pltpu.SemaphoreType.DMA((ways, chan_size - 1, count)),
            pltpu.SemaphoreType.DMA((ways, chan_size - 1, count)),
            pltpu.SemaphoreType.DMA(stack_copies),
            pltpu.SemaphoreType.DMA(stack_copies),
        ],
        compiler_params=pltpu.CompilerParams(
            vmem_limit_bytes=48 * 1024 * 1024, collective_id=0, has_side_effects=True
        ),
    )(pieces, local_channel, order)


def on_device(strain, sources):
    channels, windows, samples = strain.shape
    rounds, per_round = sources.shape
    total_sources = rounds * per_round
    factor = 1.0 / math.sqrt(lax.axis_size("win") * windows * samples)
    blocks = -(-samples // BLOCK)
    while blocks * windows % 16:
        blocks += 1
    depth = blocks * windows

    whitened = whiten(strain)
    padded = jnp.pad(whitened, ((0, 0), (0, 0), (0, blocks * BLOCK - samples)))
    pieces = padded.reshape(channels, windows, blocks, BLOCK)
    pieces = jnp.transpose(pieces, (0, 2, 1, 3)).reshape(channels, depth, BLOCK)

    flat_sources = sources.reshape(-1)
    per_shard = total_sources // lax.axis_size("chan")
    owner = flat_sources // channels
    position = jnp.arange(total_sources)
    earlier = (owner[None, :] == owner[:, None]) & (position[None, :] < position[:, None])
    rank = jnp.sum(earlier.astype(jnp.int32), axis=1)
    me = lax.axis_index("chan")
    mine = owner == me
    slot_pick = (mine[None, :] & (rank[None, :] == jnp.arange(per_shard)[:, None])).astype(jnp.int32)
    local_channel = jnp.sum(slot_pick * (flat_sources - me * channels)[None, :], axis=1)
    order = (owner * per_shard + rank).astype(jnp.int32)

    return correlate(pieces, local_channel.astype(jnp.int32), order, windows, rounds, factor)


def solution(mesh):
    in_specs = (P("chan", "win", None), P())
    out_specs = P("win", "chan", None)
    return jax.shard_map(
        on_device, mesh=mesh, in_specs=in_specs, out_specs=out_specs, check_vma=False
    )
```

```python
import functools
import math

import jax
import jax.numpy as jnp
from jax import lax
from jax.experimental import pallas as pl
from jax.experimental.pallas import tpu as pltpu
from jax.sharding import PartitionSpec as P

MAX_LAG = 256
BLOCK = 128


def whiten(strain):
    mean_square = jnp.mean(strain * strain, axis=-1, keepdims=True)
    return (strain * lax.rsqrt(mean_square + 1e-06)).astype(jnp.bfloat16)


def ring_position(index, size):
    odd = lax.rem(index, 2)
    half = index // 2
    return (1 - odd) * half + odd * (size - 1 - half)


def ring_index(position, size):
    back = position // (size // 2)
    return (1 - back) * 2 * position + back * (2 * (size - 1 - position) + 1)


def kernel(
    sizes, streamed, factor, pieces_ref, local_ref, order_ref, out_ref,
    recv_ref, wide_ref, held_ref, own_ref, probe_ref, partial_ref, send_ref, land_ref,
    send_sem, recv_sem, stack_send_sem, stack_recv_sem,
):
    chan_size, win_size, lag_blocks, windows, front = sizes
    channels = recv_ref.shape[0]
    ways, _, count, depth, _ = held_ref.shape
    per_shard = ways * count
    here = ring_position(lax.axis_index("chan"), chan_size)
    win = lax.axis_index("win")
    right = ring_index(lax.rem(here + 1, chan_size), chan_size)
    left = ring_index(lax.rem(here + chan_size - 1, chan_size), chan_size)
    targets = [right, left]

    barrier = pltpu.get_barrier_semaphore()
    for chan in targets:
        pl.semaphore_signal(barrier, inc=1, device_id={"chan": chan}, device_id_type=pl.DeviceIdType.MESH)
    for step in range(1, win_size):
        peer = lax.rem(win + step, win_size)
        pl.semaphore_signal(barrier, inc=1, device_id={"win": peer}, device_id_type=pl.DeviceIdType.MESH)
    for way in range(ways):
        for item in range(count):
            held_ref[way, 0, item] = pieces_ref[local_ref[way * count + item]]
    pl.semaphore_wait(barrier, len(targets) + win_size - 1)

    row = lax.broadcasted_iota(jnp.int32, (BLOCK, BLOCK), 0)
    lane = lax.broadcasted_iota(jnp.int32, (BLOCK, BLOCK), 1)
    later = row + lane >= BLOCK - 1
    diagonal = row + lane == BLOCK - 1

    def hop(way, step, item):
        return pltpu.make_async_remote_copy(
            src_ref=held_ref.at[way, step, item],
            dst_ref=held_ref.at[way, step + 1, item],
            send_sem=send_sem.at[way, step, item],
            recv_sem=recv_sem.at[way, step, item],
            device_id={"chan": targets[way]},
            device_id_type=pl.DeviceIdType.MESH,
        )

    def stack_hop(dest, origin):
        slot = lax.rem(dest - win + win_size, win_size) - 1
        return pltpu.make_async_remote_copy(
            src_ref=partial_ref.at[origin * per_shard + dest],
            dst_ref=land_ref.at[slot, origin],
            send_sem=stack_send_sem.at[dest, origin],
            recv_sem=stack_recv_sem.at[slot, origin],
            device_id={"win": jnp.int32(dest)},
            device_id_type=pl.DeviceIdType.MESH,
        )

    def origin_of(way, step):
        position = here - step if way == 0 else here + step
        return ring_index(lax.rem(position + chan_size, chan_size), chan_size)

    def load(probe, item, step):
        for way in range(ways):
            probe[item, :depth, way * BLOCK : (way + 1) * BLOCK] = held_ref[way, step, item]

    def work(probe, item, step, channel):
        products = jnp.dot(recv_ref[channel], probe[item], preferred_element_type=jnp.float32)
        for way in range(ways):
            columns = products[:, way * BLOCK : (way + 1) * BLOCK]
            parts = [columns[k * BLOCK : (k + 1) * BLOCK] for k in range(lag_blocks + 1)]
            totals = []
            for k in range(lag_blocks):
                mixed = jnp.where(later, parts[k], parts[k + 1])
                sheared = pltpu.roll(mixed, 0, 1, stride=1, stride_axis=0)
                total = jnp.sum(sheared, axis=0, keepdims=True)
                totals.append(pltpu.roll(total, 1, 1) * factor)
            last = jnp.where(diagonal, parts[lag_blocks], 0.0)
            last = jnp.sum(jnp.sum(last, axis=0, keepdims=True), axis=1, keepdims=True)
            totals.append(jnp.broadcast_to(last * factor, (1, BLOCK)))
            place = origin_of(way, step) * per_shard + way * count + item
            partial_ref[place, pl.ds(channel, 1), :] = jnp.concatenate(totals, axis=1)

    def send_stacks(item, step):
        if not streamed:
            return
        for way in range(ways):
            dest = way * count + item

            @pl.when(win != dest)
            def _():
                stack_hop(dest, origin_of(way, step)).start()

    for way in range(ways):
        for item in range(count):
            hop(way, 0, item).start()

    reverse = jnp.where(diagonal, 1.0, 0.0).astype(jnp.bfloat16)
    inner = recv_ref.shape[2]
    reach = wide_ref.shape[1]
    for scratch in (own_ref, probe_ref):
        scratch[:, depth:, :] = jnp.zeros((count, inner - depth, ways * BLOCK), jnp.bfloat16)
    wide_ref[...] = jnp.zeros_like(wide_ref)
    for channel in range(channels):
        wide_ref[channel % 2, front : front + depth, :] = pieces_ref[channel]
        flipped = lax.dot_general(
            reverse, wide_ref[channel % 2], (((1,), (1,)), ((), ())), preferred_element_type=jnp.float32
        )
        for k in range(lag_blocks + 1):
            shift = (lag_blocks - k) * windows
            moved = pltpu.roll(flipped, reach - shift, 1) if shift else flipped
            recv_ref[channel, k * BLOCK : (k + 1) * BLOCK, :] = moved[:, :inner].astype(jnp.bfloat16)

    spread = chan_size - 1 if chan_size - 1 <= channels else 0
    for item in range(count):
        load(own_ref, item, 0)
        for channel in range(channels - spread):
            work(own_ref, item, 0, channel)

    def body(step, carry):
        for item in range(count):
            if spread:
                work(own_ref, item, 0, channels - spread + step - 1)
            for way in range(ways):
                hop(way, step - 1, item).wait_recv()

                @pl.when(step < chan_size - 1)
                def _():
                    hop(way, step, item).start()

            load(probe_ref, item, step)
            for channel in range(channels):
                work(probe_ref, item, step, channel)
            send_stacks(item, step)
        return carry

    lax.fori_loop(1, chan_size, body, 0)
    for item in range(count):
        send_stacks(item, 0)
    for step in range(chan_size - 1):
        for way in range(ways):
            for item in range(count):
                hop(way, step, item).wait_send()

    per_win = out_ref.shape[0]
    if streamed:
        def arrived(index, carry):
            for slot in range(win_size - 1):
                peer = lax.rem(win + slot + 1, win_size)
                pltpu.make_async_remote_copy(
                    src_ref=partial_ref.at[index],
                    dst_ref=land_ref.at[slot, index],
                    send_sem=stack_send_sem.at[slot, index],
                    recv_sem=stack_recv_sem.at[slot, index],
                    device_id={"win": peer},
                    device_id_type=pl.DeviceIdType.MESH,
                ).wait_recv()
            return carry

        lax.fori_loop(0, chan_size, arrived, 0)
        for item in range(per_win):
            place = order_ref[win * per_win + item]
            owner = lax.div(place, per_shard)
            total = partial_ref[place]
            for slot in range(win_size - 1):
                total = total + land_ref[slot, owner]
            out_ref[item] = total[:, : out_ref.shape[2]]

        def sent(index, carry):
            for dest in range(win_size):
                @pl.when(win != dest)
                def _():
                    stack_hop(dest, index).wait_send()
            return carry

        lax.fori_loop(0, chan_size, sent, 0)
        return

    for dest in range(win_size):
        for item in range(per_win):
            send_ref[dest, item] = partial_ref[order_ref[dest * per_win + item]]

    def stack_copy(step):
        peer = lax.rem(win + step, win_size)
        return pltpu.make_async_remote_copy(
            src_ref=send_ref.at[peer],
            dst_ref=land_ref.at[step - 1],
            send_sem=stack_send_sem.at[step - 1],
            recv_sem=stack_recv_sem.at[step - 1],
            device_id={"win": peer},
            device_id_type=pl.DeviceIdType.MESH,
        )

    for step in range(1, win_size):
        stack_copy(step).start()
    for step in range(1, win_size):
        stack_copy(step).wait_recv()
    total = send_ref[win]
    for step in range(1, win_size):
        total = total + land_ref[step - 1]
    out_ref[...] = total[:, :, : out_ref.shape[2]]
    for step in range(1, win_size):
        stack_copy(step).wait_send()


def correlate(pieces, local_channel, order, windows, rounds, factor):
    channels, depth, _ = pieces.shape
    per_shard = local_channel.shape[0]
    total = order.shape[0]
    chan_size, win_size = lax.axis_size("chan"), lax.axis_size("win")
    lag_blocks = 2 * MAX_LAG // BLOCK
    lag_count = 2 * MAX_LAG + 1
    front = (lag_blocks - MAX_LAG // BLOCK) * windows
    inner = -(-depth // 256) * 256
    reach = -(-(inner + lag_blocks * windows) // BLOCK) * BLOCK
    lanes = (lag_blocks + 1) * BLOCK
    per_win = total // win_size
    streamed = rounds == win_size and total // rounds == chan_size and per_shard == rounds
    stack_copies = (win_size, chan_size) if streamed else (win_size - 1,)
    ways = 2 if per_shard % 2 == 0 else 1
    count = per_shard // ways
    return pl.pallas_call(
        functools.partial(kernel, (chan_size, win_size, lag_blocks, windows, front), streamed, factor),
        out_shape=jax.ShapeDtypeStruct((per_win, channels, lag_count), jnp.float32),
        in_specs=[
            pl.BlockSpec(memory_space=pltpu.VMEM),
            pl.BlockSpec(memory_space=pltpu.SMEM),
            pl.BlockSpec(memory_space=pltpu.SMEM),
        ],
        out_specs=pl.BlockSpec(memory_space=pltpu.VMEM),
        scratch_shapes=[
            pltpu.VMEM((channels, (lag_blocks + 1) * BLOCK, inner), jnp.bfloat16),
            pltpu.VMEM((2, reach, BLOCK), jnp.bfloat16),
            pltpu.VMEM((ways, chan_size, count, depth, BLOCK), jnp.bfloat16),
            pltpu.VMEM((count, inner, ways * BLOCK), jnp.bfloat16),
            pltpu.VMEM((count, inner, ways * BLOCK), jnp.bfloat16),
            pltpu.VMEM((total, channels, lanes), jnp.float32),
            pltpu.VMEM((win_size, per_win, channels, lanes), jnp.float32),
            pltpu.VMEM((win_size - 1, per_win, channels, lanes), jnp.float32),
            pltpu.SemaphoreType.DMA((ways, chan_size - 1, count)),
            pltpu.SemaphoreType.DMA((ways, chan_size - 1, count)),
            pltpu.SemaphoreType.DMA(stack_copies),
            pltpu.SemaphoreType.DMA(stack_copies),
        ],
        compiler_params=pltpu.CompilerParams(
            vmem_limit_bytes=48 * 1024 * 1024, collective_id=0, has_side_effects=True
        ),
    )(pieces, local_channel, order)


def on_device(strain, sources):
    channels, windows, samples = strain.shape
    rounds, per_round = sources.shape
    total_sources = rounds * per_round
    factor = 1.0 / math.sqrt(lax.axis_size("win") * windows * samples)
    blocks = -(-samples // BLOCK)
    while blocks * windows % 16:
        blocks += 1
    depth = blocks * windows

    whitened = whiten(strain)
    padded = jnp.pad(whitened, ((0, 0), (0, 0), (0, blocks * BLOCK - samples)))
    pieces = padded.reshape(channels, windows, blocks, BLOCK)
    pieces = jnp.transpose(pieces, (0, 2, 1, 3)).reshape(channels, depth, BLOCK)

    flat_sources = sources.reshape(-1)
    per_shard = total_sources // lax.axis_size("chan")
    owner = flat_sources // channels
    position = jnp.arange(total_sources)
    earlier = (owner[None, :] == owner[:, None]) & (position[None, :] < position[:, None])
    rank = jnp.sum(earlier.astype(jnp.int32), axis=1)
    me = lax.axis_index("chan")
    mine = owner == me
    slot_pick = (mine[None, :] & (rank[None, :] == jnp.arange(per_shard)[:, None])).astype(jnp.int32)
    local_channel = jnp.sum(slot_pick * (flat_sources - me * channels)[None, :], axis=1)
    order = (owner * per_shard + rank).astype(jnp.int32)

    return correlate(pieces, local_channel.astype(jnp.int32), order, windows, rounds, factor)


def solution(mesh):
    in_specs = (P("chan", "win", None), P())
    out_specs = P("win", "chan", None)
    return jax.shard_map(
        on_device, mesh=mesh, in_specs=in_specs, out_specs=out_specs, check_vma=False
    )
```
